32 devices in a mesh: ctx: 16 (over z, y, core), tp: 2 (over x).
Axes of the slice: x: 2, y: 2, z: 4, core: 2. Of those that a mesh axis runs over, the one named last changes fastest.
Arguments:
- tokens: bfloat16 [8192, 5376], P('ctx'), may hold values from -6 to 6
- query_weight: bfloat16 [5376, 2048], P('ctx', 'tp'), may hold values from -0.078125 to 0.078125
- key_matrix: bfloat16 [5376, 1024], P('ctx', 'tp'), may hold values from -0.078125 to 0.078125
- value_matrix: bfloat16 [5376, 1024], P('ctx', 'tp'), may hold values from -0.078125 to 0.078125
- query_gain: float32 [128], replicated, may hold values from 0.5 to 2.5
- key_norm_gain: float32 [128], replicated, may hold values from 0.5 to 2.5
- cotangent: bfloat16 [8192, 2048], P('ctx', 'tp'), may hold values from -24 to 24
Outputs:
- attended: bfloat16 [8192, 2048], P('ctx', 'tp')
- token_gradient: bfloat16 [8192, 5376], P('ctx', 'tp')
- query_gradient: bfloat16 [5376, 2048], P('ctx', 'tp')
- key_weight_gradient: bfloat16 [5376, 1024], P('ctx', 'tp')
- value_weight_gradient: bfloat16 [5376, 1024], P('ctx', 'tp')
The draws below stay inside these ranges and needn't reach their ends.
All inputs are finite; a program needn't handle non-finite values.
Results may differ from the reference program's by a relative error of at most 0.035.
Values may be sent and summed in bfloat16 or wider, within the bound.
A program may use at most 128 MiB of HBM per device.

```python
import math
import jax
import jax.numpy as jnp
from jax import lax

MODEL_WIDTH = 5376
QUERY_HEADS = 16
KEY_VALUE_HEADS = 8
HEAD_WIDTH = 128
WINDOW_LENGTH = 1024
QUERY_SCALAR = 168
TOK_DEV = 512
TOKEN_COUNT = 8192
N_CTX = 16
N_TP = 2


def spiked(values, own_key, source, target, parts, factor):
    owner, partner = [(jnp.arange(values.shape[axis_at]) // (values.shape[axis_at] // parts)).reshape([-1 if axis == axis_at else 1 for axis in range(values.ndim)]) for axis_at in (source, target)]
    chosen = jax.random.permutation(own_key, parts)[partner]
    strong = (owner == chosen) | (owner == (partner + parts // 2) % parts)
    return jnp.where(strong, factor * values, values)


def levels(stream_key, extent, shards, low, largest):
    factor_of = 1.0
    for position, blocks in shards:
        heights = jax.random.uniform(jax.random.fold_in(jax.random.fold_in(stream_key, 6), position), (blocks,), jnp.float32, low / len(shards), largest / len(shards))
        factor_of = factor_of * jnp.repeat(jnp.exp(heights), extent[position] // blocks).reshape((-1,) + (1,) * (len(extent) - 1 - position))
    return factor_of


def gaussian(own_key, shape, deviation, bound, pieces=(), kind=jnp.bfloat16):
    drawn = jax.random.normal(own_key, shape, jnp.float32) * deviation
    if len(pieces) > 0:
        drawn = levels(own_key, shape, pieces, -0.22, 0.18) * drawn
    return jnp.clip(drawn, min=-bound, max=bound).astype(kind)


def heavy_noise(key, extent, deviation, limit, split, heavy, kind=jnp.bfloat16):
    array = deviation * jax.random.normal(key, extent, jnp.float32)
    if split:
        array = array * levels(key, extent, split, -0.22, 0.18)
    return jnp.clip(spiked(array, jax.random.fold_in(key, 3), *heavy), -limit, limit).astype(kind)


def setup_inputs(seed: int = 0) -> dict:
    streams_of = jax.random.split(jax.random.key(seed), 8)
    return {
        "tokens": heavy_noise(streams_of[0], (TOKEN_COUNT, MODEL_WIDTH), 1.0, 6.0, ((0, 16),), (0, 1, 16, 2.0)),
        "query_weight": gaussian(streams_of[1], (MODEL_WIDTH, QUERY_HEADS * HEAD_WIDTH), MODEL_WIDTH ** -0.5, 0.078125, ((0, 16), (1, 2))),
        "key_matrix": gaussian(streams_of[2], (MODEL_WIDTH, KEY_VALUE_HEADS * HEAD_WIDTH), MODEL_WIDTH ** -0.5, 0.078125, ((0, 16), (1, 2))),
        "value_matrix": gaussian(streams_of[3], (MODEL_WIDTH, KEY_VALUE_HEADS * HEAD_WIDTH), MODEL_WIDTH ** -0.5, 0.078125, ((0, 16), (1, 2))),
        "query_gain": jnp.clip(jnp.exp(jax.random.uniform(streams_of[4], (HEAD_WIDTH,), jnp.float32, math.log(0.5), math.log(2.5))), 0.5, 2.5),
        "key_norm_gain": jnp.clip(jnp.exp(jax.random.uniform(streams_of[5], (HEAD_WIDTH,), jnp.float32, math.log(0.5), math.log(2.5))), 0.5, 2.5),
        "cotangent": gaussian(streams_of[6], (TOKEN_COUNT, QUERY_HEADS * HEAD_WIDTH), 4.0, 24.0, ((0, 16), (1, 2))),
    }


rope_base = 10000.0
norm_eps = 1e-06

def normalize_and_rotate(unnormed_rows, gain_vector, token_positions, head_count, head_size):
    row_total = unnormed_rows.shape[0]
    shaped = unnormed_rows.reshape(row_total, head_count, head_size)
    mean_square = lax.optimization_barrier(jnp.mean(shaped * shaped, axis=-1, keepdims=True))
    normed = shaped * lax.rsqrt(mean_square + norm_eps) * gain_vector
    half_size = head_size // 2
    inverse = jnp.power(jnp.float32(rope_base), -jnp.arange(0, head_size, 2).astype(jnp.float32) / head_size)
    angles = token_positions[:, None] * inverse[None, :]
    cosine = jnp.cos(angles)[:, None, :]
    sine_part = jnp.sin(angles)[:, None, :]
    leading = normed[..., :half_size]
    trailing = normed[..., half_size:]
    turned = jnp.concatenate([leading * cosine - trailing * sine_part, trailing * cosine + leading * sine_part], axis=-1)
    return turned.reshape(row_total, head_count * head_size)

def band_attention(query_rows, key_row_block, value_row_block, output_rows, first_query, first_key, score_scale):
    query_wide = query_rows.astype(jnp.float32)
    key_wide = key_row_block.astype(jnp.float32)
    value_wide = value_row_block.astype(jnp.float32)
    out_wide = output_rows.astype(jnp.float32)
    scores = jnp.einsum('tkgd,ckd->kgtc', query_wide, key_wide) * score_scale
    query_place = first_query + jnp.arange(query_rows.shape[0])
    key_place = first_key + jnp.arange(key_row_block.shape[0])
    visible = (key_place[None, :] >= 0) & (key_place[None, :] <= query_place[:, None]) & (key_place[None, :] > query_place[:, None] - WINDOW_LENGTH)
    exponent_terms = jnp.where(visible, jnp.exp(scores), 0.0)
    totals = lax.optimization_barrier(jnp.sum(exponent_terms, axis=-1, keepdims=True))
    probs = exponent_terms / totals
    weights = probs.astype(jnp.bfloat16)
    weight_wide = lax.optimization_barrier(weights).astype(jnp.float32)
    mixed = jnp.einsum('kgtc,ckd->tkgd', weight_wide, value_wide)
    attended = mixed.astype(jnp.bfloat16)
    delta = lax.optimization_barrier(jnp.sum(out_wide * lax.optimization_barrier(attended).astype(jnp.float32), axis=-1))
    delta = jnp.transpose(delta, (1, 2, 0))[..., None]
    prob_grads = jnp.einsum('tkgd,ckd->kgtc', out_wide, value_wide)
    score_grads = (probs * (prob_grads - delta)).astype(jnp.bfloat16)
    score_wide = lax.optimization_barrier(score_grads).astype(jnp.float32)
    query_grads = jnp.einsum('kgtc,ckd->tkgd', score_wide, key_wide) * score_scale
    key_grads = jnp.einsum('kgtc,tkgd->ckd', score_wide, query_wide) * score_scale
    value_grads = jnp.einsum('kgtc,tkgd->ckd', weight_wide, out_wide)
    return (attended, query_grads, key_grads, value_grads)

def reference(tokens, query_weight, key_matrix, value_matrix, query_gain, key_norm_gain, cotangent):
    group_width = QUERY_HEADS // KEY_VALUE_HEADS
    score_scale = QUERY_SCALAR ** (-0.5)
    token_positions = jnp.arange(TOKEN_COUNT).astype(jnp.float32)
    query_raw = jnp.dot(tokens, query_weight, preferred_element_type=jnp.float32)
    key_raw = jnp.dot(tokens, key_matrix, preferred_element_type=jnp.float32)
    value_unprojected = jnp.dot(tokens, value_matrix, preferred_element_type=jnp.float32)

    def rotate_queries(unnormed_rows):
        return normalize_and_rotate(unnormed_rows, query_gain, token_positions, QUERY_HEADS, HEAD_WIDTH)

    def rotate_keys(unnormed_rows):
        return normalize_and_rotate(unnormed_rows, key_norm_gain, token_positions, KEY_VALUE_HEADS, HEAD_WIDTH)
    query_after_rotation, query_pull = jax.vjp(rotate_queries, query_raw)
    key_after_rotation, key_pullback = jax.vjp(rotate_keys, key_raw)
    query_rows = query_after_rotation.astype(jnp.bfloat16).reshape(TOKEN_COUNT, KEY_VALUE_HEADS, group_width, HEAD_WIDTH)
    key_row_block = key_after_rotation.astype(jnp.bfloat16).reshape(TOKEN_COUNT, KEY_VALUE_HEADS, HEAD_WIDTH)
    value_row_block = value_unprojected.astype(jnp.bfloat16).reshape(TOKEN_COUNT, KEY_VALUE_HEADS, HEAD_WIDTH)
    output_rows = cotangent.reshape(TOKEN_COUNT, KEY_VALUE_HEADS, group_width, HEAD_WIDTH)
    key_rows_padded = jnp.concatenate([jnp.zeros((WINDOW_LENGTH, KEY_VALUE_HEADS, HEAD_WIDTH), jnp.bfloat16), key_row_block], axis=0)
    value_rows_padded = jnp.concatenate([jnp.zeros((WINDOW_LENGTH, KEY_VALUE_HEADS, HEAD_WIDTH), jnp.bfloat16), value_row_block], axis=0)
    span = WINDOW_LENGTH + TOK_DEV

    def block_step(carried, block_index):
        key_gradient_sums, value_gradient_sums = carried
        start_row = (block_index * TOK_DEV).astype(jnp.int32)
        query_block = lax.dynamic_slice_in_dim(query_rows, start_row, TOK_DEV, 0)
        out_block = lax.dynamic_slice_in_dim(output_rows, start_row, TOK_DEV, 0)
        key_block = lax.dynamic_slice_in_dim(key_rows_padded, start_row, span, 0)
        value_block = lax.dynamic_slice_in_dim(value_rows_padded, start_row, span, 0)
        attended, query_grads, key_grads, value_grads = band_attention(query_block, key_block, value_block, out_block, start_row, start_row - WINDOW_LENGTH, score_scale)
        key_gradient_sums = lax.dynamic_update_slice_in_dim(key_gradient_sums, lax.dynamic_slice_in_dim(key_gradient_sums, start_row, span, 0) + key_grads, start_row, 0)
        value_gradient_sums = lax.dynamic_update_slice_in_dim(value_gradient_sums, lax.dynamic_slice_in_dim(value_gradient_sums, start_row, span, 0) + value_grads, start_row, 0)
        return ((key_gradient_sums, value_gradient_sums), (attended, query_grads))
    initial_zero_sums = jnp.zeros((TOKEN_COUNT + WINDOW_LENGTH, KEY_VALUE_HEADS, HEAD_WIDTH), jnp.float32)
    (key_gradient_sums, value_gradient_sums), (attended_blocks, query_blocks) = lax.scan(block_step, (initial_zero_sums, initial_zero_sums), jnp.arange(N_CTX, dtype=jnp.int32))
    attended = attended_blocks.reshape(TOKEN_COUNT, QUERY_HEADS * HEAD_WIDTH)
    query_back, = query_pull(query_blocks.reshape(TOKEN_COUNT, QUERY_HEADS * HEAD_WIDTH))
    key_backprop, = key_pullback(key_gradient_sums[WINDOW_LENGTH:].reshape(TOKEN_COUNT, KEY_VALUE_HEADS * HEAD_WIDTH))
    query_back = query_back.astype(jnp.bfloat16)
    key_backprop = key_backprop.astype(jnp.bfloat16)
    value_backprop = value_gradient_sums[WINDOW_LENGTH:].reshape(TOKEN_COUNT, KEY_VALUE_HEADS * HEAD_WIDTH).astype(jnp.bfloat16)
    query_cols = QUERY_HEADS * HEAD_WIDTH // N_TP
    key_column_list = KEY_VALUE_HEADS * HEAD_WIDTH // N_TP
    token_sum = jnp.zeros((TOKEN_COUNT, MODEL_WIDTH), jnp.float32)
    for group_index in range(N_TP):
        query_part = slice(group_index * query_cols, (group_index + 1) * query_cols)
        key_part = slice(group_index * key_column_list, (group_index + 1) * key_column_list)
        term_value = jnp.dot(query_back[:, query_part], query_weight[:, query_part].T, preferred_element_type=jnp.float32)
        term_value = term_value + jnp.dot(key_backprop[:, key_part], key_matrix[:, key_part].T, preferred_element_type=jnp.float32)
        term_value = term_value + jnp.dot(value_backprop[:, key_part], value_matrix[:, key_part].T, preferred_element_type=jnp.float32)
        token_sum = token_sum + lax.optimization_barrier(term_value.astype(jnp.bfloat16)).astype(jnp.float32)
    token_gradient = token_sum.astype(jnp.bfloat16)
    back_rows = jnp.concatenate([query_back, key_backprop, value_backprop], axis=1)

    def block_adder(block_index, running):
        start_row = (block_index * TOK_DEV).astype(jnp.int32)
        token_block = lax.dynamic_slice_in_dim(tokens, start_row, TOK_DEV, 0)
        back_block = lax.dynamic_slice_in_dim(back_rows, start_row, TOK_DEV, 0)
        term_value = lax.dot_general(token_block, back_block, (((0,), (0,)), ((), ())), preferred_element_type=jnp.float32)
        return running + lax.optimization_barrier(term_value.astype(jnp.bfloat16)).astype(jnp.float32)
    summed_weight = lax.fori_loop(0, N_CTX, block_adder, jnp.zeros((MODEL_WIDTH, (QUERY_HEADS + 2 * KEY_VALUE_HEADS) * HEAD_WIDTH), jnp.float32))
    query_gradient = summed_weight[:, :QUERY_HEADS * HEAD_WIDTH].astype(jnp.bfloat16)
    key_weight_gradient = summed_weight[:, QUERY_HEADS * HEAD_WIDTH:(QUERY_HEADS + KEY_VALUE_HEADS) * HEAD_WIDTH].astype(jnp.bfloat16)
    value_weight_gradient = summed_weight[:, (QUERY_HEADS + KEY_VALUE_HEADS) * HEAD_WIDTH:].astype(jnp.bfloat16)
    return (attended, token_gradient, query_gradient, key_weight_gradient, value_weight_gradient)
```

```python
import functools

import jax
import jax.numpy as jnp
from jax import lax
from jax.experimental import pallas as pl
from jax.experimental.pallas import tpu as pltpu
from jax.sharding import PartitionSpec as P

HEAD_WIDTH = 128
WINDOW_LENGTH = 1024
QUERY_SCALAR = 168


rope_base = 10000.0
norm_eps = 1e-06


MESH = pl.DeviceIdType.MESH


def ring_place(size):
    chips = size // 2
    depth = chips // 2
    me = lax.axis_index("ctx")
    core = lax.rem(me, 2)
    chip = lax.div(me, 2)
    z, y = lax.div(chip, 2), lax.rem(chip, 2)
    place = z + y * (2 * depth - 1 - 2 * z)

    def at(offset, other=False):
        spot = lax.rem(place + offset + chips, chips)
        turned = lax.div(spot, depth)
        row = spot + turned * (2 * depth - 1 - 2 * spot)
        return (row * 2 + turned) * 2 + (1 - core if other else core)

    return me, chips, at


def meet(devices):
    barrier = pltpu.get_barrier_semaphore()
    for device in devices:
        pl.semaphore_signal(barrier, inc=1, device_id={"ctx": device}, device_id_type=MESH)
    pl.semaphore_wait(barrier, len(devices))


def ring_streams(chips):
    far = chips // 2
    return ((0, 1, far), (0, -1, far - 1), (1, -1, far), (1, 1, far - 1))


def gather_kernel(
    size, shard_ref, whole_ref, own_sem, own_send, own_recv, send_sem, recv_sem, side_send, side_recv
):
    me, chips, at = ring_place(size)
    half = shard_ref.shape[1] // 2
    sibling = at(0, True)
    streams = ring_streams(chips)
    meet((at(1), at(-1), sibling))

    def part(owner, which):
        return whole_ref.at[owner, :, pl.ds(which * half, half)]

    def send(src, dst, one, two, device):
        copy = pltpu.make_async_remote_copy(
            src_ref=src, dst_ref=dst, send_sem=one, recv_sem=two,
            device_id={"ctx": device}, device_id_type=MESH,
        )
        copy.start()
        return copy

    started = {}
    for k, (which, way, hops) in enumerate(streams):
        started[k, 0] = send(
            shard_ref.at[:, pl.ds(which * half, half)], part(me, which),
            send_sem.at[k, 0], recv_sem.at[k, 0], at(way),
        )
    aside = [send(shard_ref, whole_ref.at[me], own_send, own_recv, sibling)]
    mine = pltpu.make_async_copy(shard_ref, whole_ref.at[me], own_sem)
    mine.start()
    for step in range(chips // 2):
        for k, (which, way, hops) in enumerate(streams):
            if step >= hops:
                continue
            started[k, step].wait_recv()
            block = part(at(-way * (step + 1)), which)
            if step + 1 < hops:
                started[k, step + 1] = send(
                    block, block, send_sem.at[k, step + 1], recv_sem.at[k, step + 1], at(way)
                )
            aside.append(send(block, block, side_send.at[k, step], side_recv.at[k, step], sibling))
    mine.wait()
    for copy in started.values():
        copy.wait_send()
    for copy in aside:
        copy.wait()


def ring_gather(shard, collective_id):
    size = lax.axis_size("ctx")
    far = size // 4
    dma = pltpu.SemaphoreType.DMA
    return pl.pallas_call(
        functools.partial(gather_kernel, size),
        out_shape=jax.ShapeDtypeStruct((size,) + shard.shape, shard.dtype),
        in_specs=[pl.BlockSpec(memory_space=pl.ANY)],
        out_specs=pl.BlockSpec(memory_space=pl.ANY),
        scratch_shapes=[dma, dma, dma] + [dma((4, far))] * 4,
        compiler_params=pltpu.CompilerParams(collective_id=collective_id, has_side_effects=True),
        cost_estimate=pl.CostEstimate(
            flops=0, bytes_accessed=8 * size * shard.size * 2, transcendentals=0
        ),
    )(shard)


def scatter_kernel(
    size, turned_ref, back_ref, out_ref, own, mailed, arrived, passing,
    side_send, side_recv, send_sem, recv_sem,
):
    me, chips, at = ring_place(size)
    half = out_ref.shape[1] // 2
    far = chips // 2
    sibling = at(0, True)
    streams = ring_streams(chips)
    order = [far]
    for distance in range(far - 1, 0, -1):
        order += [distance, -distance]
    order += [0]
    slot_of = {offset: slot for slot, offset in enumerate(order)}
    slot_of[-far] = slot_of[far]
    meet((at(1), at(-1), sibling))

    def term(owner, target, slot):
        for which in range(2):
            target[slot, which] = jnp.dot(
                turned_ref[owner],
                back_ref[:, which * half : (which + 1) * half],
                preferred_element_type=jnp.float32,
            ).astype(jnp.bfloat16)

    sides = []

    def compute(offset):
        slot = slot_of[offset]
        term(at(offset, True), mailed, slot)
        copy = pltpu.make_async_remote_copy(
            src_ref=mailed.at[slot], dst_ref=arrived.at[slot],
            send_sem=side_send.at[slot], recv_sem=side_recv.at[slot],
            device_id={"ctx": sibling}, device_id_type=MESH,
        )
        copy.start()
        sides.append(copy)
        term(at(offset), own, slot)

    landed = set()

    def pair_sum(offset, which):
        slot = slot_of[offset]
        if slot not in landed:
            sides[slot].wait_recv()
            landed.add(slot)
        return own[slot, which].astype(jnp.float32) + arrived[slot, which].astype(jnp.float32)

    started = {}
    done = 0
    for step in range(far):
        needed = 1 + 2 * min(step + 1, far - 1)
        while done < needed:
            compute(order[done])
            done += 1
        for k, (which, way, hops) in enumerate(streams):
            if step >= hops:
                continue
            offset = way * (hops - step)
            total = pair_sum(offset, which)
            if step:
                started[k, step - 1].wait_recv()
                source = passing.at[k, step - 1]
                total = total + source[...].astype(jnp.float32)
            else:
                source = own.at[slot_of[offset], which]
            source[...] = total.astype(jnp.bfloat16)
            copy = pltpu.make_async_remote_copy(
                src_ref=source, dst_ref=passing.at[k, step],
                send_sem=send_sem.at[k, step], recv_sem=recv_sem.at[k, step],
                device_id={"ctx": at(way)}, device_id_type=MESH,
            )
            copy.start()
            started[k, step] = copy
    while done < chips:
        compute(order[done])
        done += 1
    for which in range(2):
        total = pair_sum(0, which)
        for k, (column, way, hops) in enumerate(streams):
            if column == which:
                started[k, hops - 1].wait_recv()
                total = total + passing[k, hops - 1].astype(jnp.float32)
        out_ref[:, which * half : (which + 1) * half] = total.astype(jnp.bfloat16)
    for copy in sides:
        copy.wait_send()
    for copy in started.values():
        copy.wait_send()


def weight_gradient(turned, back, collective_id):
    size = lax.axis_size("ctx")
    chips = size // 2
    far = chips // 2
    rows, columns = turned.shape[1], back.shape[1]
    half = columns // 2
    dma = pltpu.SemaphoreType.DMA
    vmem = pl.BlockSpec(memory_space=pltpu.VMEM)
    block = (2, rows, half)
    return pl.pallas_call(
        functools.partial(scatter_kernel, size),
        out_shape=jax.ShapeDtypeStruct((rows, columns), jnp.bfloat16),
        in_specs=[vmem, vmem],
        out_specs=vmem,
        scratch_shapes=[pltpu.VMEM((chips,) + block, jnp.bfloat16)] * 3
        + [pltpu.VMEM((4, far, rows, half), jnp.bfloat16)]
        + [dma((chips,))] * 2
        + [dma((4, far))] * 2,
        compiler_params=pltpu.CompilerParams(
            collective_id=collective_id, has_side_effects=True, vmem_limit_bytes=56 * 2**20
        ),
        cost_estimate=pl.CostEstimate(
            flops=2 * turned.size * columns, bytes_accessed=8 * size * rows * columns * 2,
            transcendentals=0,
        ),
    )(turned, back)


def passed_along(shard, axis, by):
    size = lax.axis_size(axis)
    pairs = [(i, i + by) for i in range(size) if 0 <= i + by < size]
    return lax.ppermute(shard, axis, pairs)


def normalize_and_rotate(unnormed_rows, gain_vector, token_positions, head_count, head_size):
    row_total = unnormed_rows.shape[0]
    shaped = unnormed_rows.reshape(row_total, head_count, head_size)
    mean_square = jnp.mean(shaped * shaped, axis=-1, keepdims=True)
    normed = shaped * lax.rsqrt(mean_square + norm_eps) * gain_vector
    half_size = head_size // 2
    inverse = jnp.power(
        jnp.float32(rope_base), -jnp.arange(0, head_size, 2).astype(jnp.float32) / head_size
    )
    angles = token_positions[:, None] * inverse[None, :]
    cosine = jnp.cos(angles)[:, None, :]
    sine_part = jnp.sin(angles)[:, None, :]
    leading = normed[..., :half_size]
    trailing = normed[..., half_size:]
    turned = jnp.concatenate(
        [leading * cosine - trailing * sine_part, trailing * cosine + leading * sine_part], axis=-1
    )
    return turned.reshape(row_total, head_count * head_size)


def band_attention(
    query_rows, key_row_block, value_row_block, output_rows, first_query, first_key, score_scale
):
    scores = (
        jnp.einsum("tkgd,ckd->kgtc", query_rows, key_row_block, preferred_element_type=jnp.float32)
        * score_scale
    )
    query_place = first_query + jnp.arange(query_rows.shape[0], dtype=jnp.int32)
    key_place = first_key + jnp.arange(key_row_block.shape[0], dtype=jnp.int32)
    visible = (
        (key_place[None, :] >= 0)
        & (key_place[None, :] <= query_place[:, None])
        & (key_place[None, :] > query_place[:, None] - WINDOW_LENGTH)
    )
    exponent_terms = jnp.where(visible, jnp.exp(scores), 0.0)
    totals = jnp.sum(exponent_terms, axis=-1, keepdims=True)
    probs = exponent_terms / totals
    weights = probs.astype(jnp.bfloat16)
    mixed = jnp.einsum(
        "kgtc,ckd->tkgd", weights, value_row_block, preferred_element_type=jnp.float32
    )
    attended = mixed.astype(jnp.bfloat16)
    delta = jnp.sum(
        output_rows.astype(jnp.float32) * lax.optimization_barrier(attended).astype(jnp.float32),
        axis=-1,
    )
    delta = jnp.transpose(delta, (1, 2, 0))[..., None]
    prob_grads = jnp.einsum(
        "tkgd,ckd->kgtc", output_rows, value_row_block, preferred_element_type=jnp.float32
    )
    score_grads = (probs * (prob_grads - delta)).astype(jnp.bfloat16)
    query_grads = (
        jnp.einsum("kgtc,ckd->tkgd", score_grads, key_row_block, preferred_element_type=jnp.float32)
        * score_scale
    )
    key_grads = (
        jnp.einsum("kgtc,tkgd->ckd", score_grads, query_rows, preferred_element_type=jnp.float32)
        * score_scale
    )
    value_grads = jnp.einsum(
        "kgtc,tkgd->ckd", weights, output_rows, preferred_element_type=jnp.float32
    )
    return (attended, query_grads, key_grads, value_grads)


def transposed(left_rows, right_rows):
    return lax.dot_general(
        left_rows, right_rows, (((1,), (1,)), ((), ())), preferred_element_type=jnp.float32
    )


def shards(tokens, query_weight, key_matrix, value_matrix, query_gain, key_norm_gain, cotangent):
    row_count = tokens.shape[0]
    heads_query = query_weight.shape[1] // HEAD_WIDTH
    heads_key = key_matrix.shape[1] // HEAD_WIDTH
    group_width = heads_query // heads_key
    reach_back = WINDOW_LENGTH // row_count
    score_scale = QUERY_SCALAR ** (-0.5)
    first_row = lax.axis_index("ctx") * row_count
    token_positions = (first_row + jnp.arange(row_count, dtype=jnp.int32)).astype(jnp.float32)
    key_columns = key_matrix.shape[1]
    width = tokens.shape[1]
    size = lax.axis_size("ctx")
    full_pair = ring_gather(jnp.concatenate([key_matrix, value_matrix], axis=1), 1)
    flat_pair = full_pair.reshape(width, 2 * key_columns)
    pair_raw = jnp.dot(tokens, flat_pair, preferred_element_type=jnp.float32)
    key_raw, value_unprojected = pair_raw[:, :key_columns], pair_raw[:, key_columns:]
    turned_tokens = tokens.T.reshape(size, width // size, row_count)

    def rotate_queries(unnormed_rows):
        return normalize_and_rotate(
            unnormed_rows, query_gain, token_positions, heads_query, HEAD_WIDTH
        )

    def rotate_keys(unnormed_rows):
        return normalize_and_rotate(
            unnormed_rows, key_norm_gain, token_positions, heads_key, HEAD_WIDTH
        )

    key_after_rotation, key_pullback = jax.vjp(rotate_keys, key_raw)
    stacked = jnp.stack(
        [
            key_after_rotation.astype(jnp.bfloat16).reshape(row_count, heads_key, HEAD_WIDTH),
            value_unprojected.astype(jnp.bfloat16).reshape(row_count, heads_key, HEAD_WIDTH),
        ]
    )
    arrivals = [passed_along(stacked, "ctx", by) for by in range(1, reach_back + 1)]
    query_weight, stacked = lax.optimization_barrier((query_weight, stacked))
    full_query = ring_gather(query_weight, 2)
    flat_query = full_query.reshape(width, query_weight.shape[1])
    query_raw = jnp.dot(tokens, flat_query, preferred_element_type=jnp.float32)
    query_after_rotation, query_pull = jax.vjp(rotate_queries, query_raw)
    query_rows = query_after_rotation.astype(jnp.bfloat16).reshape(
        row_count, heads_key, group_width, HEAD_WIDTH
    )
    band_rows = jnp.concatenate(arrivals[::-1] + [stacked], axis=1)
    output_rows = cotangent.reshape(row_count, heads_key, group_width, HEAD_WIDTH)
    attended, query_grads, key_grads, value_grads = band_attention(
        query_rows,
        band_rows[0],
        band_rows[1],
        output_rows,
        first_row,
        first_row - WINDOW_LENGTH,
        score_scale,
    )
    band_grads = jnp.stack([key_grads, value_grads])

    def band_tile(distance):
        lowest = (reach_back - distance) * row_count
        return band_grads[:, lowest : lowest + row_count]

    (query_back,) = query_pull(query_grads.reshape(row_count, heads_query * HEAD_WIDTH))
    query_back = query_back.astype(jnp.bfloat16)
    returned = band_tile(0)
    for by in range(1, reach_back + 1):
        returned = returned + passed_along(
            band_tile(by).astype(jnp.bfloat16), "ctx", -by
        ).astype(jnp.float32)
    query_gradient = weight_gradient(turned_tokens, query_back, 3)
    (key_backprop,) = key_pullback(returned[0].reshape(row_count, heads_key * HEAD_WIDTH))
    key_backprop = key_backprop.astype(jnp.bfloat16)
    value_backprop = returned[1].reshape(row_count, heads_key * HEAD_WIDTH).astype(jnp.bfloat16)
    pair_back = jnp.concatenate([key_backprop, value_backprop], axis=1)
    pair_back, query_gradient = lax.optimization_barrier((pair_back, query_gradient))

    def token_terms(query_part, pair_part):
        return (transposed(query_back, query_part) + transposed(pair_back, pair_part)).astype(
            jnp.bfloat16
        )

    if lax.axis_size("tp") == 2:
        group = lax.axis_index("tp")
        query_halves = flat_query.reshape(2, width // 2, -1)
        pair_halves = flat_pair.reshape(2, width // 2, -1)

        def half_terms(which):
            return token_terms(
                lax.dynamic_index_in_dim(query_halves, which, 0, False),
                lax.dynamic_index_in_dim(pair_halves, which, 0, False),
            )

        given = lax.ppermute(half_terms(1 - group), "tp", [(0, 1), (1, 0)])
        pair_gradient = weight_gradient(turned_tokens, pair_back, 4)
        token_gradient = (
            half_terms(group).astype(jnp.float32) + given.astype(jnp.float32)
        ).astype(jnp.bfloat16)
    else:
        token_gradient = lax.psum_scatter(
            token_terms(flat_query, flat_pair), "tp", scatter_dimension=1, tiled=True
        )
        pair_gradient = weight_gradient(turned_tokens, pair_back, 4)
    return (
        attended.reshape(row_count, heads_query * HEAD_WIDTH),
        token_gradient,
        query_gradient,
        pair_gradient[:, :key_columns],
        pair_gradient[:, key_columns:],
    )


def solution(mesh):
    in_specs = (
        P("ctx", None),
        P("ctx", "tp"),
        P("ctx", "tp"),
        P("ctx", "tp"),
        P(),
        P(),
        P("ctx", "tp"),
    )
    out_specs = (P("ctx", "tp"), P("ctx", "tp"), P("ctx", "tp"), P("ctx", "tp"), P("ctx", "tp"))
    return jax.shard_map(shards, mesh=mesh, in_specs=in_specs, out_specs=out_specs, check_vma=False)
```

```python
import functools

import jax
import jax.numpy as jnp
from jax import lax
from jax.experimental import pallas as pl
from jax.experimental.pallas import tpu as pltpu
from jax.sharding import PartitionSpec as P

HEAD_WIDTH = 128
WINDOW_LENGTH = 1024
QUERY_SCALAR = 168


rope_base = 10000.0
norm_eps = 1e-06


MESH = pl.DeviceIdType.MESH
MAIL_SLOTS = 3


def ring_place(size):
    chips = size // 2
    depth = chips // 2
    me = lax.axis_index("ctx")
    core = lax.rem(me, 2)
    chip = lax.div(me, 2)
    z, y = lax.div(chip, 2), lax.rem(chip, 2)
    place = z + y * (2 * depth - 1 - 2 * z)

    def at(offset, other=False):
        spot = lax.rem(place + offset + chips, chips)
        turned = lax.div(spot, depth)
        row = spot + turned * (2 * depth - 1 - 2 * spot)
        return (row * 2 + turned) * 2 + (1 - core if other else core)

    return me, chips, at


def meet(devices):
    barrier = pltpu.get_barrier_semaphore()
    for device in devices:
        pl.semaphore_signal(barrier, inc=1, device_id={"ctx": device}, device_id_type=MESH)
    pl.semaphore_wait(barrier, len(devices))


def ring_streams(chips):
    far = chips // 2
    return ((0, 1, far), (0, -1, far - 1), (1, -1, far), (1, 1, far - 1))


def project_kernel(
    size, shard_ref, turned_ref, full_ref, raw_ref, whole_ref,
    own_sem, out_sem, own_send, own_recv, send_sem, recv_sem, side_send, side_recv,
):
    me, chips, at = ring_place(size)
    half = shard_ref.shape[1] // 2
    sibling = at(0, True)
    streams = ring_streams(chips)
    meet((at(1), at(-1), sibling))

    def part(owner, which):
        return whole_ref.at[owner, :, pl.ds(which * half, half)]

    def send(src, dst, one, two, device):
        copy = pltpu.make_async_remote_copy(
            src_ref=src, dst_ref=dst, send_sem=one, recv_sem=two,
            device_id={"ctx": device}, device_id_type=MESH,
        )
        copy.start()
        return copy

    written = []

    def multiply(owner, which):
        columns = slice(which * half, (which + 1) * half)
        raw_ref[:, columns] += lax.dot_general(
            turned_ref[owner], whole_ref[owner, :, columns], (((0,), (0,)), ((), ())),
            preferred_element_type=jnp.float32,
        )
        keep = pltpu.make_async_copy(
            part(owner, which), full_ref.at[owner, :, pl.ds(which * half, half)],
            out_sem.at[len(written)],
        )
        keep.start()
        written.append(keep)

    started = {}
    for k, (which, way, hops) in enumerate(streams):
        started[k, 0] = send(
            shard_ref.at[:, pl.ds(which * half, half)], part(me, which),
            send_sem.at[k, 0], recv_sem.at[k, 0], at(way),
        )
    own_side = send(shard_ref, whole_ref.at[me], own_send, own_recv, sibling)
    mine = pltpu.make_async_copy(shard_ref, whole_ref.at[me], own_sem)
    mine.start()
    raw_ref[...] = jnp.zeros_like(raw_ref)
    mine.wait()
    for which in range(2):
        multiply(me, which)
    own_side.wait_recv()
    for which in range(2):
        multiply(sibling, which)
    aside = []
    waiting = []
    for step in range(chips // 2):
        here = []
        for k, (which, way, hops) in enumerate(streams):
            if step >= hops:
                continue
            started[k, step].wait_recv()
            block = part(at(-way * (step + 1)), which)
            if step + 1 < hops:
                started[k, step + 1] = send(
                    block, block, send_sem.at[k, step + 1], recv_sem.at[k, step + 1], at(way)
                )
            copy = send(block, block, side_send.at[k, step], side_recv.at[k, step], sibling)
            aside.append(copy)
            here.append((copy, -way * (step + 1), which))
        for copy, offset, which in waiting:
            copy.wait_recv()
            multiply(at(offset, True), which)
        for _, offset, which in here:
            multiply(at(offset), which)
        waiting = here
    for copy, offset, which in waiting:
        copy.wait_recv()
        multiply(at(offset, True), which)
    for keep in written:
        keep.wait()
    own_side.wait_send()
    for copy in list(started.values()) + aside:
        copy.wait_send()


def gather_and_project(shard, turned, collective_id):
    size = lax.axis_size("ctx")
    far = size // 4
    dma = pltpu.SemaphoreType.DMA
    whole = (size,) + shard.shape
    vmem = pl.BlockSpec(memory_space=pltpu.VMEM)
    return pl.pallas_call(
        functools.partial(project_kernel, size),
        out_shape=(
            jax.ShapeDtypeStruct(whole, shard.dtype),
            jax.ShapeDtypeStruct((turned.shape[2], shard.shape[1]), jnp.float32),
        ),
        in_specs=[vmem, vmem],
        out_specs=(pl.BlockSpec(memory_space=pl.ANY), vmem),
        scratch_shapes=[pltpu.VMEM(whole, shard.dtype), dma, dma((2 * size,)), dma, dma]
        + [dma((4, far))] * 4,
        compiler_params=pltpu.CompilerParams(
            collective_id=collective_id, has_side_effects=True, vmem_limit_bytes=58 * 2**20
        ),
        cost_estimate=pl.CostEstimate(
            flops=2 * turned.size * shard.shape[1], bytes_accessed=8 * size * shard.size * 2,
            transcendentals=0,
        ),
    )(shard, turned)


def scatter_kernel(
    size, turned_ref, back_ref, out_ref, own, mailed, arrived, passing,
    side_send, side_recv, send_sem, recv_sem,
):
    me, chips, at = ring_place(size)
    half = out_ref.shape[1] // 2
    far = chips // 2
    sibling = at(0, True)
    streams = ring_streams(chips)
    order = [far]
    for distance in range(far - 1, 0, -1):
        order += [distance, -distance]
    order += [0]
    slot_of = {offset: slot for slot, offset in enumerate(order)}
    slot_of[-far] = slot_of[far]
    meet((at(1), at(-1), sibling))

    def term(owner, target, slot):
        for which in range(2):
            target[slot, which] = jnp.dot(
                turned_ref[owner],
                back_ref[:, which * half : (which + 1) * half],
                preferred_element_type=jnp.float32,
            ).astype(jnp.bfloat16)

    sides = []

    def compute(offset):
        slot = slot_of[offset]
        if slot >= MAIL_SLOTS:
            sides[slot - MAIL_SLOTS].wait_send()
        term(at(offset, True), mailed, slot % MAIL_SLOTS)
        copy = pltpu.make_async_remote_copy(
            src_ref=mailed.at[slot % MAIL_SLOTS], dst_ref=arrived.at[slot],
            send_sem=side_send.at[slot], recv_sem=side_recv.at[slot],
            device_id={"ctx": sibling}, device_id_type=MESH,
        )
        copy.start()
        sides.append(copy)
        term(at(offset), own, slot)

    landed = set()

    def pair_sum(offset, which):
        slot = slot_of[offset]
        if slot not in landed:
            sides[slot].wait_recv()
            landed.add(slot)
        return own[slot, which].astype(jnp.float32) + arrived[slot, which].astype(jnp.float32)

    started = {}
    done = 0
    for step in range(far):
        needed = 1 + 2 * min(step + 1, far - 1)
        while done < needed:
            compute(order[done])
            done += 1
        for k, (which, way, hops) in enumerate(streams):
            if step >= hops:
                continue
            offset = way * (hops - step)
            total = pair_sum(offset, which)
            if step:
                started[k, step - 1].wait_recv()
                source = passing.at[k, step - 1]
                total = total + source[...].astype(jnp.float32)
            else:
                source = own.at[slot_of[offset], which]
            source[...] = total.astype(jnp.bfloat16)
            copy = pltpu.make_async_remote_copy(
                src_ref=source, dst_ref=passing.at[k, step],
                send_sem=send_sem.at[k, step], recv_sem=recv_sem.at[k, step],
                device_id={"ctx": at(way)}, device_id_type=MESH,
            )
            copy.start()
            started[k, step] = copy
    while done < chips:
        compute(order[done])
        done += 1
    for which in range(2):
        total = pair_sum(0, which)
        for k, (column, way, hops) in enumerate(streams):
            if column == which:
                started[k, hops - 1].wait_recv()
                total = total + passing[k, hops - 1].astype(jnp.float32)
        out_ref[:, which * half : (which + 1) * half] = total.astype(jnp.bfloat16)
    for copy in sides[-MAIL_SLOTS:]:
        copy.wait_send()
    for copy in started.values():
        copy.wait_send()


def weight_gradient(turned, back, collective_id):
    size = lax.axis_size("ctx")
    chips = size // 2
    far = chips // 2
    rows, columns = turned.shape[1], back.shape[1]
    half = columns // 2
    dma = pltpu.SemaphoreType.DMA
    vmem = pl.BlockSpec(memory_space=pltpu.VMEM)
    block = (2, rows, half)
    return pl.pallas_call(
        functools.partial(scatter_kernel, size),
        out_shape=jax.ShapeDtypeStruct((rows, columns), jnp.bfloat16),
        in_specs=[vmem, vmem],
        out_specs=vmem,
        scratch_shapes=[pltpu.VMEM((chips,) + block, jnp.bfloat16)]
        + [pltpu.VMEM((MAIL_SLOTS,) + block, jnp.bfloat16)]
        + [pltpu.VMEM((chips,) + block, jnp.bfloat16)]
        + [pltpu.VMEM((4, far, rows, half), jnp.bfloat16)]
        + [dma((chips,))] * 2
        + [dma((4, far))] * 2,
        compiler_params=pltpu.CompilerParams(
            collective_id=collective_id, has_side_effects=True, vmem_limit_bytes=58 * 2**20
        ),
        cost_estimate=pl.CostEstimate(
            flops=2 * turned.size * columns, bytes_accessed=8 * size * rows * columns * 2,
            transcendentals=0,
        ),
    )(turned, back)


def passed_along(shard, axis, by):
    size = lax.axis_size(axis)
    pairs = [(i, i + by) for i in range(size) if 0 <= i + by < size]
    return lax.ppermute(shard, axis, pairs)


def normalize_and_rotate(unnormed_rows, gain_vector, token_positions, head_count, head_size):
    row_total = unnormed_rows.shape[0]
    shaped = unnormed_rows.reshape(row_total, head_count, head_size)
    mean_square = jnp.mean(shaped * shaped, axis=-1, keepdims=True)
    normed = shaped * lax.rsqrt(mean_square + norm_eps) * gain_vector
    half_size = head_size // 2
    inverse = jnp.power(
        jnp.float32(rope_base), -jnp.arange(0, head_size, 2).astype(jnp.float32) / head_size
    )
    angles = token_positions[:, None] * inverse[None, :]
    cosine = jnp.cos(angles)[:, None, :]
    sine_part = jnp.sin(angles)[:, None, :]
    leading = normed[..., :half_size]
    trailing = normed[..., half_size:]
    turned = jnp.concatenate(
        [leading * cosine - trailing * sine_part, trailing * cosine + leading * sine_part], axis=-1
    )
    return turned.reshape(row_total, head_count * head_size)


def attention_kernel(
    raw_ref, key_ref, value_ref, out_ref, cos_ref, sin_ref, gain_ref,
    attended_ref, back_ref, key_grad_ref, value_grad_ref,
):
    rows = raw_ref.shape[0]
    group = raw_ref.shape[1] // HEAD_WIDTH
    tile = min(rows, 256)
    span = tile + WINDOW_LENGTH
    scale = QUERY_SCALAR ** (-0.5)
    log2_e = 1.4426950408889634
    first_row = lax.axis_index("ctx") * rows
    gain = gain_ref[...]
    key_grad_ref[...] = jnp.zeros_like(key_grad_ref)
    value_grad_ref[...] = jnp.zeros_like(value_grad_ref)
    place = lax.broadcasted_iota(jnp.int32, (1, span), 1)
    row = lax.rem(lax.broadcasted_iota(jnp.int32, (group * tile, tile), 0), tile)
    column = lax.broadcasted_iota(jnp.int32, (group * tile, tile), 1)
    newer = column > row

    def contract(left, right, dims):
        return lax.dot_general(left, right, (dims, ((), ())), preferred_element_type=jnp.float32)

    def heads(ref, rows_here):
        return jnp.concatenate(
            [ref[rows_here, g * HEAD_WIDTH : (g + 1) * HEAD_WIDTH] for g in range(group)], axis=0
        )

    for start in range(0, rows, tile):
        here = slice(start, start + tile)
        band = slice(start, start + span)
        cosine = jnp.concatenate([cos_ref[here, :]] * group, axis=0)
        sine = jnp.concatenate([sin_ref[here, :]] * group, axis=0)
        raw = heads(raw_ref, here)
        shrink = lax.rsqrt(jnp.mean(raw * raw, axis=-1, keepdims=True) + norm_eps)
        normed = raw * shrink * gain
        query = (normed * cosine + pltpu.roll(normed, HEAD_WIDTH // 2, 1) * sine).astype(
            jnp.bfloat16
        )
        keys = key_ref[band, :]
        values = value_ref[band, :]
        given = heads(out_ref, here)
        bias = jnp.where(place + (start - WINDOW_LENGTH) + first_row >= 0, 0.0, -1e30)
        terms = jnp.exp2(contract(query, keys, ((1,), (1,))) * (scale * log2_e) + bias)
        terms = jnp.concatenate(
            [
                jnp.where(newer, terms[:, :tile], 0.0),
                terms[:, tile : span - tile],
                jnp.where(newer, 0.0, terms[:, span - tile :]),
            ],
            axis=1,
        )
        probs = terms * (1.0 / jnp.sum(terms, axis=-1, keepdims=True))
        weights = probs.astype(jnp.bfloat16)
        attended = contract(weights, values, ((1,), (0,))).astype(jnp.bfloat16)
        delta = jnp.sum(
            given.astype(jnp.float32) * attended.astype(jnp.float32), axis=-1, keepdims=True
        )
        prob_grads = contract(given, values, ((1,), (1,)))
        score_grads = (probs * (prob_grads - delta)).astype(jnp.bfloat16)
        grads = contract(score_grads, keys, ((1,), (0,))) * scale
        key_grad_ref[band, :] += contract(score_grads, query, ((0,), (0,))) * scale
        value_grad_ref[band, :] += contract(weights, given, ((0,), (0,)))
        unturned = grads * cosine + pltpu.roll(grads * sine, HEAD_WIDTH // 2, 1)
        scaled = unturned * gain
        back = shrink * (
            scaled
            - raw * (shrink * shrink) * jnp.mean(raw * scaled, axis=-1, keepdims=True)
        )
        for g in range(group):
            lanes = slice(g * HEAD_WIDTH, (g + 1) * HEAD_WIDTH)
            those = slice(g * tile, (g + 1) * tile)
            attended_ref[here, lanes] = attended[those]
            back_ref[here, lanes] = back[those].astype(jnp.bfloat16)


def band_attention(query_raw, band_rows, output_rows, cosine, sine, gain, heads_key):
    rows, width = query_raw.shape
    span = band_rows.shape[0]
    wide = width // heads_key
    queries = pl.BlockSpec((rows, wide), lambda g: (0, g))
    keys = pl.BlockSpec((span, HEAD_WIDTH), lambda g: (0, g))
    values = pl.BlockSpec((span, HEAD_WIDTH), lambda g: (0, heads_key + g))
    table = pl.BlockSpec((rows, HEAD_WIDTH), lambda g: (0, 0))
    return pl.pallas_call(
        attention_kernel,
        grid=(heads_key,),
        out_shape=(
            jax.ShapeDtypeStruct((rows, width), jnp.bfloat16),
            jax.ShapeDtypeStruct((rows, width), jnp.bfloat16),
            jax.ShapeDtypeStruct((span, heads_key * HEAD_WIDTH), jnp.float32),
            jax.ShapeDtypeStruct((span, heads_key * HEAD_WIDTH), jnp.float32),
        ),
        in_specs=[
            queries, keys, values, queries, table, table,
            pl.BlockSpec((1, HEAD_WIDTH), lambda g: (0, 0)),
        ],
        out_specs=(queries, queries, keys, keys),
        compiler_params=pltpu.CompilerParams(vmem_limit_bytes=56 * 2**20),
        cost_estimate=pl.CostEstimate(
            flops=10 * rows * span * width, bytes_accessed=16 * rows * width,
            transcendentals=rows * span * (width // HEAD_WIDTH),
        ),
    )(query_raw, band_rows, band_rows, output_rows, cosine, sine, gain)


def transposed(left_rows, right_rows):
    return lax.dot_general(
        left_rows, right_rows, (((1,), (1,)), ((), ())), preferred_element_type=jnp.float32
    )


def shards(tokens, query_weight, key_matrix, value_matrix, query_gain, key_norm_gain, cotangent):
    row_count = tokens.shape[0]
    heads_key = key_matrix.shape[1] // HEAD_WIDTH
    reach_back = WINDOW_LENGTH // row_count
    first_row = lax.axis_index("ctx") * row_count
    token_positions = (first_row + jnp.arange(row_count, dtype=jnp.int32)).astype(jnp.float32)
    query_columns, key_columns = query_weight.shape[1], key_matrix.shape[1]
    width = tokens.shape[1]
    size = lax.axis_size("ctx")
    turned_tokens = tokens.T.reshape(size, width // size, row_count)
    shard = jnp.concatenate([query_weight, key_matrix, value_matrix], axis=1)
    full_weight, raw = gather_and_project(shard, turned_tokens, 1)
    flat_weight = full_weight.reshape(width, shard.shape[1])
    query_raw = raw[:, :query_columns]
    key_raw = raw[:, query_columns : query_columns + key_columns]
    value_rows = raw[:, query_columns + key_columns :].astype(jnp.bfloat16)

    inverse = jnp.power(
        jnp.float32(rope_base),
        -jnp.arange(0, HEAD_WIDTH, 2).astype(jnp.float32) / HEAD_WIDTH,
    )
    angles = token_positions[:, None] * inverse[None, :]
    cosine, sine = jnp.cos(angles), jnp.sin(angles)
    cosine = jnp.concatenate([cosine, cosine], axis=1)
    sine = jnp.concatenate([-sine, sine], axis=1)

    def rotate_keys(unnormed_rows):
        return normalize_and_rotate(
            unnormed_rows, key_norm_gain, token_positions, heads_key, HEAD_WIDTH
        )

    key_after_rotation, key_pullback = jax.vjp(rotate_keys, key_raw)
    stacked = jnp.concatenate([key_after_rotation.astype(jnp.bfloat16), value_rows], axis=1)
    arrivals = []
    carried = stacked
    for hop_count in range(reach_back):
        carried = passed_along(carried, "ctx", 1)
        arrivals.append(carried)
    band_rows = jnp.concatenate(arrivals[::-1] + [stacked], axis=0)
    attended, query_back, key_grads, value_grads = band_attention(
        query_raw, band_rows, cotangent, cosine, sine, query_gain[None, :], heads_key
    )

    def band_tile(distance):
        lowest = (reach_back - distance) * row_count
        rows_here = slice(lowest, lowest + row_count)
        return jnp.concatenate([key_grads[rows_here], value_grads[rows_here]], axis=1)

    returned = band_tile(reach_back)
    for hop_count in range(1, reach_back + 1):
        returned = passed_along(returned.astype(jnp.bfloat16), "ctx", -1).astype(
            jnp.float32
        ) + band_tile(reach_back - hop_count)
    (key_backprop,) = key_pullback(returned[:, :key_columns])
    pair_back = jnp.concatenate([key_backprop, returned[:, key_columns:]], axis=1).astype(
        jnp.bfloat16
    )
    all_back = jnp.concatenate([query_back, pair_back], axis=1)

    def token_terms(part):
        return (
            transposed(query_back, part[:, :query_columns])
            + transposed(pair_back, part[:, query_columns:])
        ).astype(jnp.bfloat16)

    if lax.axis_size("tp") == 2:
        group = lax.axis_index("tp")
        halves = flat_weight.reshape(2, width // 2, -1)

        def half_terms(which):
            return token_terms(lax.dynamic_index_in_dim(halves, which, 0, False))

        given = lax.ppermute(half_terms(1 - group), "tp", [(0, 1), (1, 0)])
        gradient = weight_gradient(turned_tokens, all_back, 2)
        token_gradient = (
            half_terms(group).astype(jnp.float32) + given.astype(jnp.float32)
        ).astype(jnp.bfloat16)
    else:
        token_gradient = lax.psum_scatter(
            token_terms(flat_weight), "tp", scatter_dimension=1, tiled=True
        )
        gradient = weight_gradient(turned_tokens, all_back, 2)
    return (
        attended,
        token_gradient,
        gradient[:, :query_columns],
        gradient[:, query_columns : query_columns + key_columns],
        gradient[:, query_columns + key_columns :],
    )


def solution(mesh):
    in_specs = (
        P("ctx", None),
        P("ctx", "tp"),
        P("ctx", "tp"),
        P("ctx", "tp"),
        P(),
        P(),
        P("ctx", "tp"),
    )
    out_specs = (P("ctx", "tp"), P("ctx", "tp"), P("ctx", "tp"), P("ctx", "tp"), P("ctx", "tp"))
    return jax.shard_map(shards, mesh=mesh, in_specs=in_specs, out_specs=out_specs, check_vma=False)
```

```python
import functools

import jax
import jax.numpy as jnp
from jax import lax
from jax.experimental import pallas as pl
from jax.experimental.pallas import tpu as pltpu
from jax.sharding import PartitionSpec as P

HEAD_WIDTH = 128
WINDOW_LENGTH = 1024
QUERY_SCALAR = 168


rope_base = 10000.0
norm_eps = 1e-06


MESH = pl.DeviceIdType.MESH
MAIL_SLOTS = 3
PARTS = 4


def ring_place(size):
    chips = size // 2
    depth = chips // 2
    me = lax.axis_index("ctx")
    core = lax.rem(me, 2)
    chip = lax.div(me, 2)
    z, y = lax.div(chip, 2), lax.rem(chip, 2)
    place = z + y * (2 * depth - 1 - 2 * z)

    def at(offset, other=False):
        spot = lax.rem(place + offset + chips, chips)
        turned = lax.div(spot, depth)
        row = spot + turned * (2 * depth - 1 - 2 * spot)
        return (row * 2 + turned) * 2 + (1 - core if other else core)

    return me, chips, at


def meet(devices):
    barrier = pltpu.get_barrier_semaphore()
    for device in devices:
        pl.semaphore_signal(barrier, inc=1, device_id={"ctx": device}, device_id_type=MESH)
    pl.semaphore_wait(barrier, len(devices))


def ring_streams(chips):
    far = chips // 2
    streams = []
    for first in range(PARTS // 2):
        last = first + PARTS // 2
        streams += [(first, 1, far), (last, -1, far), (first, -1, far - 1), (last, 1, far - 1)]
    return streams


def project_kernel(
    size, shard_ref, tokens_ref, full_ref, turned_ref, query_ref, key_ref, value_ref, whole_ref,
    own_sem, out_sem, own_send, own_recv, send_sem, recv_sem, side_send, side_recv,
):
    me, chips, at = ring_place(size)
    half = shard_ref.shape[1] // PARTS
    depth, rows = shard_ref.shape[0], tokens_ref.shape[0]
    sibling = at(0, True)
    streams = ring_streams(chips)
    meet((at(1), at(-1), sibling))

    def part(owner, which):
        return whole_ref.at[owner, :, pl.ds(which * half, half)]

    def send(src, dst, one, two, device):
        copy = pltpu.make_async_remote_copy(
            src_ref=src, dst_ref=dst, send_sem=one, recv_sem=two,
            device_id={"ctx": device}, device_id_type=MESH,
        )
        copy.start()
        return copy

    written = []
    shift = (1 - lax.axis_index("tp")) * (size // 2) if lax.axis_size("tp") == 2 else 0

    def multiply(owner, which):
        columns = slice(which * half, (which + 1) * half)
        raw_ref, spot = (
            (query_ref, columns), (query_ref, columns),
            (key_ref, slice(0, half)), (value_ref, slice(0, half)),
        )[which]
        raw_ref[:, spot] += lax.dot_general(
            turned_ref[owner], whole_ref[owner, :, columns], (((0,), (0,)), ((), ())),
            preferred_element_type=jnp.float32,
        )
        spot = lax.rem(owner + shift, size)
        keep = pltpu.make_async_copy(
            part(owner, which), full_ref.at[spot, :, pl.ds(which * half, half)],
            out_sem.at[len(written)],
        )
        keep.start()
        written.append(keep)

    started = {}
    for k, (which, way, hops) in enumerate(streams):
        started[k, 0] = send(
            shard_ref.at[:, pl.ds(which * half, half)], part(me, which),
            send_sem.at[k, 0], recv_sem.at[k, 0], at(way),
        )
    own_side = send(shard_ref, whole_ref.at[me], own_send, own_recv, sibling)
    mine = pltpu.make_async_copy(shard_ref, whole_ref.at[me], own_sem)
    mine.start()
    for ref in (query_ref, key_ref, value_ref):
        ref[...] = jnp.zeros_like(ref)
    for low in range(0, tokens_ref.shape[1], 128):
        piece = tokens_ref[:, low : low + 128].T
        at_row = low
        while at_row < low + 128:
            owner, inner = at_row // depth, at_row % depth
            count = min(depth - inner, low + 128 - at_row)
            turned_ref[owner, inner : inner + count, :] = piece[at_row - low : at_row - low + count]
            at_row += count
    mine.wait()
    for which in range(PARTS):
        multiply(me, which)
    own_side.wait_recv()
    for which in range(PARTS):
        multiply(sibling, which)
    aside = []
    waiting = []
    for step in range(chips // 2):
        here = []
        for k, (which, way, hops) in enumerate(streams):
            if step >= hops:
                continue
            started[k, step].wait_recv()
            block = part(at(-way * (step + 1)), which)
            if step + 1 < hops:
                started[k, step + 1] = send(
                    block, block, send_sem.at[k, step + 1], recv_sem.at[k, step + 1], at(way)
                )
            copy = send(block, block, side_send.at[k, step], side_recv.at[k, step], sibling)
            aside.append(copy)
            here.append((copy, -way * (step + 1), which))
        for copy, offset, which in waiting:
            copy.wait_recv()
            multiply(at(offset, True), which)
        for _, offset, which in here:
            multiply(at(offset), which)
        waiting = here
    for copy, offset, which in waiting:
        copy.wait_recv()
        multiply(at(offset, True), which)
    for keep in written:
        keep.wait()
    own_side.wait_send()
    for copy in list(started.values()) + aside:
        copy.wait_send()


def gather_and_project(shard, tokens, collective_id):
    size = lax.axis_size("ctx")
    far = size // 4
    dma = pltpu.SemaphoreType.DMA
    whole = (size,) + shard.shape
    rows, quarter = tokens.shape[0], shard.shape[1] // PARTS
    vmem = pl.BlockSpec(memory_space=pltpu.VMEM)
    return pl.pallas_call(
        functools.partial(project_kernel, size),
        out_shape=(
            jax.ShapeDtypeStruct(whole, shard.dtype),
            jax.ShapeDtypeStruct((size, shard.shape[0], rows), tokens.dtype),
            jax.ShapeDtypeStruct((rows, 2 * quarter), jnp.float32),
            jax.ShapeDtypeStruct((rows, quarter), jnp.float32),
            jax.ShapeDtypeStruct((rows, quarter), jnp.float32),
        ),
        in_specs=[vmem, vmem],
        out_specs=(pl.BlockSpec(memory_space=pl.ANY), vmem, vmem, vmem, vmem),
        scratch_shapes=[pltpu.VMEM(whole, shard.dtype), dma, dma((PARTS * size,)), dma, dma]
        + [dma((2 * PARTS, far))] * 4,
        compiler_params=pltpu.CompilerParams(
            collective_id=collective_id, has_side_effects=True, vmem_limit_bytes=58 * 2**20
        ),
        cost_estimate=pl.CostEstimate(
            flops=2 * tokens.size * shard.shape[1], bytes_accessed=8 * size * shard.size * 2,
            transcendentals=0,
        ),
    )(shard, tokens)


def scatter_kernel(
    size, turned_ref, back_ref, out_ref, own, mailed, arrived, passing,
    side_send, side_recv, send_sem, recv_sem,
):
    me, chips, at = ring_place(size)
    half = out_ref.shape[1] // PARTS
    far = chips // 2
    sibling = at(0, True)
    streams = ring_streams(chips)
    order = [far]
    for distance in range(far - 1, 0, -1):
        order += [distance, -distance]
    order += [0]
    slot_of = {offset: slot for slot, offset in enumerate(order)}
    slot_of[-far] = slot_of[far]
    meet((at(1), at(-1), sibling))

    def term(owner, target, slot):
        for which in range(PARTS):
            target[slot, which] = jnp.dot(
                turned_ref[owner],
                back_ref[:, which * half : (which + 1) * half],
                preferred_element_type=jnp.float32,
            ).astype(jnp.bfloat16)

    sides = []

    def compute(offset):
        slot = slot_of[offset]
        if slot >= MAIL_SLOTS:
            sides[slot - MAIL_SLOTS].wait_send()
        term(at(offset, True), mailed, slot % MAIL_SLOTS)
        copy = pltpu.make_async_remote_copy(
            src_ref=mailed.at[slot % MAIL_SLOTS], dst_ref=arrived.at[slot],
            send_sem=side_send.at[slot], recv_sem=side_recv.at[slot],
            device_id={"ctx": sibling}, device_id_type=MESH,
        )
        copy.start()
        sides.append(copy)
        term(at(offset), own, slot)

    landed = set()

    def pair_sum(offset, which):
        slot = slot_of[offset]
        if slot not in landed:
            sides[slot].wait_recv()
            landed.add(slot)
        return own[slot, which].astype(jnp.float32) + arrived[slot, which].astype(jnp.float32)

    started = {}
    done = 0
    turns = [(step, hops) for step in range(far) for hops in (far, far - 1)]
    for step, length in turns:
        needed = 1 + 2 * (step if length == far else min(step + 1, far - 1))
        while done < needed:
            compute(order[done])
            done += 1
        for k, (which, way, hops) in enumerate(streams):
            if step >= hops or hops != length:
                continue
            offset = way * (hops - step)
            total = pair_sum(offset, which)
            if step:
                started[k, step - 1].wait_recv()
                source = passing.at[k, step - 1]
                total = total + source[...].astype(jnp.float32)
            else:
                source = own.at[slot_of[offset], which]
            source[...] = total.astype(jnp.bfloat16)
            copy = pltpu.make_async_remote_copy(
                src_ref=source, dst_ref=passing.at[k, step],
                send_sem=send_sem.at[k, step], recv_sem=recv_sem.at[k, step],
                device_id={"ctx": at(way)}, device_id_type=MESH,
            )
            copy.start()
            started[k, step] = copy
    while done < chips:
        compute(order[done])
        done += 1
    for which in range(PARTS):
        total = pair_sum(0, which)
        for k, (column, way, hops) in enumerate(streams):
            if column == which:
                started[k, hops - 1].wait_recv()
                total = total + passing[k, hops - 1].astype(jnp.float32)
        out_ref[:, which * half : (which + 1) * half] = total.astype(jnp.bfloat16)
    for copy in sides[-MAIL_SLOTS:]:
        copy.wait_send()
    for copy in started.values():
        copy.wait_send()


def weight_gradient(turned, back, collective_id):
    size = lax.axis_size("ctx")
    chips = size // 2
    far = chips // 2
    rows, columns = turned.shape[1], back.shape[1]
    half = columns // PARTS
    dma = pltpu.SemaphoreType.DMA
    vmem = pl.BlockSpec(memory_space=pltpu.VMEM)
    block = (PARTS, rows, half)
    return pl.pallas_call(
        functools.partial(scatter_kernel, size),
        out_shape=jax.ShapeDtypeStruct((rows, columns), jnp.bfloat16),
        in_specs=[vmem, vmem],
        out_specs=vmem,
        scratch_shapes=[pltpu.VMEM((chips,) + block, jnp.bfloat16)]
        + [pltpu.VMEM((MAIL_SLOTS,) + block, jnp.bfloat16)]
        + [pltpu.VMEM((chips,) + block, jnp.bfloat16)]
        + [pltpu.VMEM((2 * PARTS, far, rows, half), jnp.bfloat16)]
        + [dma((chips,))] * 2
        + [dma((2 * PARTS, far))] * 2,
        compiler_params=pltpu.CompilerParams(
            collective_id=collective_id, has_side_effects=True, vmem_limit_bytes=58 * 2**20
        ),
        cost_estimate=pl.CostEstimate(
            flops=2 * turned.size * columns, bytes_accessed=8 * size * rows * columns * 2,
            transcendentals=0,
        ),
    )(turned, back)


def passed_along(shard, axis, by):
    size = lax.axis_size(axis)
    pairs = [(i, i + by) for i in range(size) if 0 <= i + by < size]
    return lax.ppermute(shard, axis, pairs)


def normalize_and_rotate(unnormed_rows, gain_vector, token_positions, head_count, head_size):
    row_total = unnormed_rows.shape[0]
    shaped = unnormed_rows.reshape(row_total, head_count, head_size)
    mean_square = jnp.mean(shaped * shaped, axis=-1, keepdims=True)
    normed = shaped * lax.rsqrt(mean_square + norm_eps) * gain_vector
    half_size = head_size // 2
    inverse = jnp.power(
        jnp.float32(rope_base), -jnp.arange(0, head_size, 2).astype(jnp.float32) / head_size
    )
    angles = token_positions[:, None] * inverse[None, :]
    cosine = jnp.cos(angles)[:, None, :]
    sine_part = jnp.sin(angles)[:, None, :]
    leading = normed[..., :half_size]
    trailing = normed[..., half_size:]
    turned = jnp.concatenate(
        [leading * cosine - trailing * sine_part, trailing * cosine + leading * sine_part], axis=-1
    )
    return turned.reshape(row_total, head_count * head_size)


def attention_kernel(
    reach_back, raw_ref, out_ref, cos_ref, sin_ref, gain_ref, *refs
):
    bands, refs = refs[: reach_back + 1], refs[reach_back + 1 :]
    attended_ref, back_ref = refs[:2]
    tiles, refs = refs[2 : reach_back + 3], refs[reach_back + 3 :]
    key_ref, value_ref, key_grad_ref, value_grad_ref = refs
    rows = raw_ref.shape[0]
    group = raw_ref.shape[1] // HEAD_WIDTH
    tile = min(rows, 256)
    span = tile + WINDOW_LENGTH
    scale = QUERY_SCALAR ** (-0.5)
    log2_e = 1.4426950408889634
    first_row = lax.axis_index("ctx") * rows
    gain = gain_ref[...]
    for index, band_ref in enumerate(bands):
        key_ref[index * rows : (index + 1) * rows, :] = band_ref[0]
        value_ref[index * rows : (index + 1) * rows, :] = band_ref[1]
    key_grad_ref[...] = jnp.zeros_like(key_grad_ref)
    value_grad_ref[...] = jnp.zeros_like(value_grad_ref)
    place = lax.broadcasted_iota(jnp.int32, (1, span), 1)
    row = lax.rem(lax.broadcasted_iota(jnp.int32, (group * tile, tile), 0), tile)
    column = lax.broadcasted_iota(jnp.int32, (group * tile, tile), 1)
    newer = column > row

    def contract(left, right, dims):
        return lax.dot_general(left, right, (dims, ((), ())), preferred_element_type=jnp.float32)

    def heads(ref, rows_here):
        return jnp.concatenate(
            [ref[rows_here, g * HEAD_WIDTH : (g + 1) * HEAD_WIDTH] for g in range(group)], axis=0
        )

    for start in range(0, rows, tile):
        here = slice(start, start + tile)
        band = slice(start, start + span)
        cosine = jnp.concatenate([cos_ref[here, :]] * group, axis=0)
        sine = jnp.concatenate([sin_ref[here, :]] * group, axis=0)
        raw = heads(raw_ref, here)
        shrink = lax.rsqrt(jnp.mean(raw * raw, axis=-1, keepdims=True) + norm_eps)
        normed = raw * shrink * gain
        query = (normed * cosine + pltpu.roll(normed, HEAD_WIDTH // 2, 1) * sine).astype(
            jnp.bfloat16
        )
        keys = key_ref[band, :]
        values = value_ref[band, :]
        given = heads(out_ref, here)
        bias = jnp.where(place + (start - WINDOW_LENGTH) + first_row >= 0, 0.0, -1e30)
        terms = jnp.exp2(contract(query, keys, ((1,), (1,))) * (scale * log2_e) + bias)
        terms = jnp.concatenate(
            [
                jnp.where(newer, terms[:, :tile], 0.0),
                terms[:, tile : span - tile],
                jnp.where(newer, 0.0, terms[:, span - tile :]),
            ],
            axis=1,
        )
        probs = terms * (1.0 / jnp.sum(terms, axis=-1, keepdims=True))
        weights = probs.astype(jnp.bfloat16)
        attended = contract(weights, values, ((1,), (0,))).astype(jnp.bfloat16)
        delta = jnp.sum(
            given.astype(jnp.float32) * attended.astype(jnp.float32), axis=-1, keepdims=True
        )
        prob_grads = contract(given, values, ((1,), (1,)))
        score_grads = (probs * (prob_grads - delta)).astype(jnp.bfloat16)
        grads = contract(score_grads, keys, ((1,), (0,))) * scale
        key_grad_ref[band, :] += contract(score_grads, query, ((0,), (0,))) * scale
        value_grad_ref[band, :] += contract(weights, given, ((0,), (0,)))
        unturned = grads * cosine + pltpu.roll(grads * sine, HEAD_WIDTH // 2, 1)
        scaled = unturned * gain
        back = shrink * (
            scaled
            - raw * (shrink * shrink) * jnp.mean(raw * scaled, axis=-1, keepdims=True)
        )
        for g in range(group):
            lanes = slice(g * HEAD_WIDTH, (g + 1) * HEAD_WIDTH)
            those = slice(g * tile, (g + 1) * tile)
            attended_ref[here, lanes] = attended[those]
            back_ref[here, lanes] = back[those].astype(jnp.bfloat16)
    for index, tile_ref in enumerate(tiles):
        for which, ref in enumerate((key_grad_ref, value_grad_ref)):
            tile_ref[which] = ref[index * rows : (index + 1) * rows, :].astype(tile_ref.dtype)


def band_attention(query_raw, bands, output_rows, cosine, sine, gain, heads_key):
    rows, width = query_raw.shape
    reach_back = len(bands) - 1
    span = rows * len(bands)
    wide = width // heads_key
    queries = pl.BlockSpec((rows, wide), lambda g: (0, g))
    pairs = pl.BlockSpec((2, rows, HEAD_WIDTH), lambda g: (0, 0, g))
    table = pl.BlockSpec((rows, HEAD_WIDTH), lambda g: (0, 0))
    kinds = [jnp.bfloat16] + [jnp.float32] * reach_back
    return pl.pallas_call(
        functools.partial(attention_kernel, reach_back),
        grid=(heads_key,),
        out_shape=[jax.ShapeDtypeStruct((rows, width), jnp.bfloat16)] * 2
        + [jax.ShapeDtypeStruct(bands[0].shape, kind) for kind in kinds],
        in_specs=[
            queries, queries, table, table, pl.BlockSpec((1, HEAD_WIDTH), lambda g: (0, 0)),
        ]
        + [pairs] * len(bands),
        out_specs=[queries, queries] + [pairs] * len(bands),
        scratch_shapes=[pltpu.VMEM((span, HEAD_WIDTH), jnp.bfloat16)] * 2
        + [pltpu.VMEM((span, HEAD_WIDTH), jnp.float32)] * 2,
        compiler_params=pltpu.CompilerParams(vmem_limit_bytes=56 * 2**20),
        cost_estimate=pl.CostEstimate(
            flops=10 * rows * span * width, bytes_accessed=16 * rows * width,
            transcendentals=rows * span * (width // HEAD_WIDTH),
        ),
    )(query_raw, output_rows, cosine, sine, gain, *bands)


def transposed(left_rows, right_rows):
    return lax.dot_general(
        left_rows, right_rows, (((1,), (1,)), ((), ())), preferred_element_type=jnp.float32
    )


def shards(tokens, query_weight, key_matrix, value_matrix, query_gain, key_norm_gain, cotangent):
    row_count = tokens.shape[0]
    heads_key = key_matrix.shape[1] // HEAD_WIDTH
    reach_back = WINDOW_LENGTH // row_count
    first_row = lax.axis_index("ctx") * row_count
    token_positions = (first_row + jnp.arange(row_count, dtype=jnp.int32)).astype(jnp.float32)
    query_columns, key_columns = query_weight.shape[1], key_matrix.shape[1]
    width = tokens.shape[1]
    size = lax.axis_size("ctx")
    shard = jnp.concatenate([query_weight, key_matrix, value_matrix], axis=1)
    full_weight, turned_tokens, query_raw, key_raw, value_raw = gather_and_project(
        shard, tokens, 1
    )
    flat_weight = full_weight.reshape(width, shard.shape[1])
    value_rows = value_raw.astype(jnp.bfloat16)

    inverse = jnp.power(
        jnp.float32(rope_base),
        -jnp.arange(0, HEAD_WIDTH, 2).astype(jnp.float32) / HEAD_WIDTH,
    )
    angles = token_positions[:, None] * inverse[None, :]
    cosine, sine = jnp.cos(angles), jnp.sin(angles)
    cosine = jnp.concatenate([cosine, cosine], axis=1)
    sine = jnp.concatenate([-sine, sine], axis=1)

    def rotate_keys(unnormed_rows):
        return normalize_and_rotate(
            unnormed_rows, key_norm_gain, token_positions, heads_key, HEAD_WIDTH
        )

    key_after_rotation, key_pullback = jax.vjp(rotate_keys, key_raw)
    stacked = jnp.stack([key_after_rotation.astype(jnp.bfloat16), value_rows])
    arrivals = []
    carried = stacked
    for hop_count in range(reach_back):
        carried = passed_along(carried, "ctx", 1)
        arrivals.append(carried)
    attended, query_back, *tiles = band_attention(
        query_raw, arrivals[::-1] + [stacked], cotangent, cosine, sine,
        query_gain[None, :], heads_key,
    )
    paired = lax.axis_size("tp") == 2
    weight_parts = [flat_weight]
    if paired:
        weight_parts = [flat_weight[: width // 2], flat_weight[width // 2 :]]
    query_terms = [transposed(query_back, part[:, :query_columns]) for part in weight_parts]
    returned = tiles[0]
    for hop_count in range(1, reach_back + 1):
        arrived = passed_along(returned.astype(jnp.bfloat16), "ctx", -1)
        if hop_count <= len(query_terms):
            arrived, query_terms[hop_count - 1] = lax.optimization_barrier(
                (arrived, query_terms[hop_count - 1])
            )
        returned = arrived.astype(jnp.float32) + tiles[hop_count]
    (key_backprop,) = key_pullback(returned[0])
    pair_back = jnp.concatenate([key_backprop, returned[1]], axis=1).astype(jnp.bfloat16)
    all_back = jnp.concatenate([query_back, pair_back], axis=1)
    token_terms = [
        (term + transposed(pair_back, part[:, query_columns:])).astype(jnp.bfloat16)
        for term, part in zip(query_terms, weight_parts)
    ]
    if paired:
        given = lax.ppermute(token_terms[0], "tp", [(0, 1), (1, 0)])
        gradient = weight_gradient(turned_tokens, all_back, 2)
        token_gradient = (
            token_terms[1].astype(jnp.float32) + given.astype(jnp.float32)
        ).astype(jnp.bfloat16)
    else:
        token_gradient = lax.psum_scatter(
            token_terms[0], "tp", scatter_dimension=1, tiled=True
        )
        gradient = weight_gradient(turned_tokens, all_back, 2)
    return (
        attended,
        token_gradient,
        gradient[:, :query_columns],
        gradient[:, query_columns : query_columns + key_columns],
        gradient[:, query_columns + key_columns :],
    )


def solution(mesh):
    in_specs = (
        P("ctx", None),
        P("ctx", "tp"),
        P("ctx", "tp"),
        P("ctx", "tp"),
        P(),
        P(),
        P("ctx", "tp"),
    )
    out_specs = (P("ctx", "tp"), P("ctx", "tp"), P("ctx", "tp"), P("ctx", "tp"), P("ctx", "tp"))
    return jax.shard_map(shards, mesh=mesh, in_specs=in_specs, out_specs=out_specs, check_vma=False)
```

```python
import functools

import jax
import jax.numpy as jnp
from jax import lax
from jax.experimental import pallas as pl
from jax.experimental.pallas import tpu as pltpu
from jax.sharding import PartitionSpec as P

HEAD_WIDTH = 128
WINDOW_LENGTH = 1024
QUERY_SCALAR = 168


rope_base = 10000.0
norm_eps = 1e-06


MESH = pl.DeviceIdType.MESH
MAIL_SLOTS = 3
PARTS = 4


def ring_place(size):
    chips = size // 2
    depth = chips // 2
    me = lax.axis_index("ctx")
    core = lax.rem(me, 2)
    chip = lax.div(me, 2)
    z, y = lax.div(chip, 2), lax.rem(chip, 2)
    place = z + y * (2 * depth - 1 - 2 * z)

    def at(offset, other=False):
        spot = lax.rem(place + offset + chips, chips)
        turned = lax.div(spot, depth)
        row = spot + turned * (2 * depth - 1 - 2 * spot)
        return (row * 2 + turned) * 2 + (1 - core if other else core)

    return me, chips, at


def meet(devices):
    barrier = pltpu.get_barrier_semaphore()
    for device in devices:
        pl.semaphore_signal(barrier, inc=1, device_id={"ctx": device}, device_id_type=MESH)
    pl.semaphore_wait(barrier, len(devices))


def ring_streams(chips):
    far = chips // 2
    streams = []
    for first in range(PARTS // 2):
        last = first + PARTS // 2
        streams += [(first, 1, far), (last, -1, far), (first, -1, far - 1), (last, 1, far - 1)]
    return streams


def project_kernel(
    size, shard_ref, tokens_ref, cos_ref, sin_ref, gain_ref,
    full_ref, turned_ref, query_ref, key_ref, value_ref, pair_ref, whole_ref,
    own_sem, out_sem, own_send, own_recv, send_sem, recv_sem, side_send, side_recv,
):
    me, chips, at = ring_place(size)
    half = shard_ref.shape[1] // PARTS
    depth, rows = shard_ref.shape[0], tokens_ref.shape[0]
    sibling = at(0, True)
    streams = ring_streams(chips)
    meet((at(1), at(-1), sibling))

    def part(owner, which):
        return whole_ref.at[owner, :, pl.ds(which * half, half)]

    def send(src, dst, one, two, device):
        copy = pltpu.make_async_remote_copy(
            src_ref=src, dst_ref=dst, send_sem=one, recv_sem=two,
            device_id={"ctx": device}, device_id_type=MESH,
        )
        copy.start()
        return copy

    written = []
    shift = (1 - lax.axis_index("tp")) * (size // 2) if lax.axis_size("tp") == 2 else 0

    def multiply(owner, which):
        columns = slice(which * half, (which + 1) * half)
        raw_ref, spot = (
            (query_ref, columns), (query_ref, columns),
            (key_ref, slice(0, half)), (value_ref, slice(0, half)),
        )[which]
        raw_ref[:, spot] += lax.dot_general(
            turned_ref[owner], whole_ref[owner, :, columns], (((0,), (0,)), ((), ())),
            preferred_element_type=jnp.float32,
        )
        spot = lax.rem(owner + shift, size)
        keep = pltpu.make_async_copy(
            part(owner, which), full_ref.at[spot, :, pl.ds(which * half, half)],
            out_sem.at[len(written)],
        )
        keep.start()
        written.append(keep)

    started = {}
    for k, (which, way, hops) in enumerate(streams):
        started[k, 0] = send(
            shard_ref.at[:, pl.ds(which * half, half)], part(me, which),
            send_sem.at[k, 0], recv_sem.at[k, 0], at(way),
        )
    own_side = send(shard_ref, whole_ref.at[me], own_send, own_recv, sibling)
    mine = pltpu.make_async_copy(shard_ref, whole_ref.at[me], own_sem)
    mine.start()
    for ref in (query_ref, key_ref, value_ref):
        ref[...] = jnp.zeros_like(ref)
    for low in range(0, tokens_ref.shape[1], 128):
        piece = tokens_ref[:, low : low + 128].T
        at_row = low
        while at_row < low + 128:
            owner, inner = at_row // depth, at_row % depth
            count = min(depth - inner, low + 128 - at_row)
            turned_ref[owner, inner : inner + count, :] = piece[at_row - low : at_row - low + count]
            at_row += count
    mine.wait()
    for which in range(PARTS):
        multiply(me, which)
    own_side.wait_recv()
    for which in range(PARTS):
        multiply(sibling, which)
    aside = []
    waiting = []
    for step in range(chips // 2):
        here = []
        for k, (which, way, hops) in enumerate(streams):
            if step >= hops:
                continue
            started[k, step].wait_recv()
            block = part(at(-way * (step + 1)), which)
            if step + 1 < hops:
                started[k, step + 1] = send(
                    block, block, send_sem.at[k, step + 1], recv_sem.at[k, step + 1], at(way)
                )
            copy = send(block, block, side_send.at[k, step], side_recv.at[k, step], sibling)
            aside.append(copy)
            here.append((copy, -way * (step + 1), which))
        for copy, offset, which in waiting:
            copy.wait_recv()
            multiply(at(offset, True), which)
        for _, offset, which in here:
            multiply(at(offset), which)
        waiting = here
    for copy, offset, which in waiting:
        copy.wait_recv()
        multiply(at(offset, True), which)
    for low in range(0, key_ref.shape[1], HEAD_WIDTH):
        lanes = slice(low, low + HEAD_WIDTH)
        raw = key_ref[:, lanes]
        normed = raw * lax.rsqrt(jnp.mean(raw * raw, axis=-1, keepdims=True) + norm_eps)
        normed = normed * gain_ref[...]
        pair_ref[0, :, lanes] = (
            normed * cos_ref[...] + pltpu.roll(normed, HEAD_WIDTH // 2, 1) * sin_ref[...]
        ).astype(jnp.bfloat16)
    pair_ref[1] = value_ref[...].astype(jnp.bfloat16)
    for keep in written:
        keep.wait()
    own_side.wait_send()
    for copy in list(started.values()) + aside:
        copy.wait_send()


def gather_and_project(shard, tokens, cosine, sine, gain, collective_id):
    size = lax.axis_size("ctx")
    far = size // 4
    dma = pltpu.SemaphoreType.DMA
    whole = (size,) + shard.shape
    rows, quarter = tokens.shape[0], shard.shape[1] // PARTS
    vmem = pl.BlockSpec(memory_space=pltpu.VMEM)
    return pl.pallas_call(
        functools.partial(project_kernel, size),
        out_shape=(
            jax.ShapeDtypeStruct(whole, shard.dtype),
            jax.ShapeDtypeStruct((size, shard.shape[0], rows), tokens.dtype),
            jax.ShapeDtypeStruct((rows, 2 * quarter), jnp.float32),
            jax.ShapeDtypeStruct((rows, quarter), jnp.float32),
            jax.ShapeDtypeStruct((rows, quarter), jnp.float32),
            jax.ShapeDtypeStruct((2, rows, quarter), jnp.bfloat16),
        ),
        in_specs=[vmem] * 5,
        out_specs=(pl.BlockSpec(memory_space=pl.ANY),) + (vmem,) * 5,
        scratch_shapes=[pltpu.VMEM(whole, shard.dtype), dma, dma((PARTS * size,)), dma, dma]
        + [dma((2 * PARTS, far))] * 4,
        compiler_params=pltpu.CompilerParams(
            collective_id=collective_id, has_side_effects=True, vmem_limit_bytes=58 * 2**20
        ),
        cost_estimate=pl.CostEstimate(
            flops=2 * tokens.size * shard.shape[1], bytes_accessed=8 * size * shard.size * 2,
            transcendentals=0,
        ),
    )(shard, tokens, cosine, sine, gain)


def scatter_kernel(
    size, turned_ref, back_ref, out_ref, own, mailed, arrived, passing,
    side_send, side_recv, send_sem, recv_sem,
):
    me, chips, at = ring_place(size)
    half = out_ref.shape[1] // PARTS
    far = chips // 2
    sibling = at(0, True)
    streams = ring_streams(chips)
    order = [far]
    for distance in range(far - 1, 0, -1):
        order += [distance, -distance]
    order += [0]
    slot_of = {offset: slot for slot, offset in enumerate(order)}
    slot_of[-far] = slot_of[far]
    meet((at(1), at(-1), sibling))

    def term(owner, target, slot):
        for which in range(PARTS):
            target[slot, which] = jnp.dot(
                turned_ref[owner],
                back_ref[:, which * half : (which + 1) * half],
                preferred_element_type=jnp.float32,
            ).astype(jnp.bfloat16)

    sides = []

    def compute(offset):
        slot = slot_of[offset]
        if slot >= MAIL_SLOTS:
            sides[slot - MAIL_SLOTS].wait_send()
        term(at(offset, True), mailed, slot % MAIL_SLOTS)
        copy = pltpu.make_async_remote_copy(
            src_ref=mailed.at[slot % MAIL_SLOTS], dst_ref=arrived.at[slot],
            send_sem=side_send.at[slot], recv_sem=side_recv.at[slot],
            device_id={"ctx": sibling}, device_id_type=MESH,
        )
        copy.start()
        sides.append(copy)
        term(at(offset), own, slot)

    landed = set()

    def pair_sum(offset, which):
        slot = slot_of[offset]
        if slot not in landed:
            sides[slot].wait_recv()
            landed.add(slot)
        return own[slot, which].astype(jnp.float32) + arrived[slot, which].astype(jnp.float32)

    started = {}
    done = 0
    turns = [(step, hops) for step in range(far) for hops in (far, far - 1)]
    for step, length in turns:
        needed = 1 + 2 * (step if length == far else min(step + 1, far - 1))
        while done < needed:
            compute(order[done])
            done += 1
        for k, (which, way, hops) in enumerate(streams):
            if step >= hops or hops != length:
                continue
            offset = way * (hops - step)
            total = pair_sum(offset, which)
            if step:
                started[k, step - 1].wait_recv()
                source = passing.at[k, step - 1]
                total = total + source[...].astype(jnp.float32)
            else:
                source = own.at[slot_of[offset], which]
            source[...] = total.astype(jnp.bfloat16)
            copy = pltpu.make_async_remote_copy(
                src_ref=source, dst_ref=passing.at[k, step],
                send_sem=send_sem.at[k, step], recv_sem=recv_sem.at[k, step],
                device_id={"ctx": at(way)}, device_id_type=MESH,
            )
            copy.start()
            started[k, step] = copy
    while done < chips:
        compute(order[done])
        done += 1
    for which in range(PARTS):
        total = pair_sum(0, which)
        for k, (column, way, hops) in enumerate(streams):
            if column == which:
                started[k, hops - 1].wait_recv()
                total = total + passing[k, hops - 1].astype(jnp.float32)
        out_ref[:, which * half : (which + 1) * half] = total.astype(jnp.bfloat16)
    for copy in sides[-MAIL_SLOTS:]:
        copy.wait_send()
    for copy in started.values():
        copy.wait_send()


def weight_gradient(turned, back, collective_id):
    size = lax.axis_size("ctx")
    chips = size // 2
    far = chips // 2
    rows, columns = turned.shape[1], back.shape[1]
    half = columns // PARTS
    dma = pltpu.SemaphoreType.DMA
    vmem = pl.BlockSpec(memory_space=pltpu.VMEM)
    block = (PARTS, rows, half)
    return pl.pallas_call(
        functools.partial(scatter_kernel, size),
        out_shape=jax.ShapeDtypeStruct((rows, columns), jnp.bfloat16),
        in_specs=[vmem, vmem],
        out_specs=vmem,
        scratch_shapes=[pltpu.VMEM((chips,) + block, jnp.bfloat16)]
        + [pltpu.VMEM((MAIL_SLOTS,) + block, jnp.bfloat16)]
        + [pltpu.VMEM((chips,) + block, jnp.bfloat16)]
        + [pltpu.VMEM((2 * PARTS, far, rows, half), jnp.bfloat16)]
        + [dma((chips,))] * 2
        + [dma((2 * PARTS, far))] * 2,
        compiler_params=pltpu.CompilerParams(
            collective_id=collective_id, has_side_effects=True, vmem_limit_bytes=58 * 2**20
        ),
        cost_estimate=pl.CostEstimate(
            flops=2 * turned.size * columns, bytes_accessed=8 * size * rows * columns * 2,
            transcendentals=0,
        ),
    )(turned, back)


def passed_along(shard, axis, by):
    size = lax.axis_size(axis)
    pairs = [(i, i + by) for i in range(size) if 0 <= i + by < size]
    return lax.ppermute(shard, axis, pairs)


def normalize_and_rotate(unnormed_rows, gain_vector, token_positions, head_count, head_size):
    row_total = unnormed_rows.shape[0]
    shaped = unnormed_rows.reshape(row_total, head_count, head_size)
    mean_square = jnp.mean(shaped * shaped, axis=-1, keepdims=True)
    normed = shaped * lax.rsqrt(mean_square + norm_eps) * gain_vector
    half_size = head_size // 2
    inverse = jnp.power(
        jnp.float32(rope_base), -jnp.arange(0, head_size, 2).astype(jnp.float32) / head_size
    )
    angles = token_positions[:, None] * inverse[None, :]
    cosine = jnp.cos(angles)[:, None, :]
    sine_part = jnp.sin(angles)[:, None, :]
    leading = normed[..., :half_size]
    trailing = normed[..., half_size:]
    turned = jnp.concatenate(
        [leading * cosine - trailing * sine_part, trailing * cosine + leading * sine_part], axis=-1
    )
    return turned.reshape(row_total, head_count * head_size)


def attention_kernel(
    reach_back, raw_ref, out_ref, cos_ref, sin_ref, gain_ref, *refs
):
    bands, refs = refs[: reach_back + 1], refs[reach_back + 1 :]
    attended_ref, back_ref = refs[:2]
    tiles, refs = refs[2 : reach_back + 3], refs[reach_back + 3 :]
    key_ref, value_ref, key_grad_ref, value_grad_ref = refs
    rows = raw_ref.shape[0]
    group = raw_ref.shape[1] // HEAD_WIDTH
    tile = min(rows, 256)
    span = tile + WINDOW_LENGTH
    scale = QUERY_SCALAR ** (-0.5)
    log2_e = 1.4426950408889634
    first_row = lax.axis_index("ctx") * rows
    gain = gain_ref[...]
    for index, band_ref in enumerate(bands):
        key_ref[index * rows : (index + 1) * rows, :] = band_ref[0]
        value_ref[index * rows : (index + 1) * rows, :] = band_ref[1]
    key_grad_ref[...] = jnp.zeros_like(key_grad_ref)
    value_grad_ref[...] = jnp.zeros_like(value_grad_ref)
    place = lax.broadcasted_iota(jnp.int32, (1, span), 1)
    row = lax.rem(lax.broadcasted_iota(jnp.int32, (group * tile, tile), 0), tile)
    column = lax.broadcasted_iota(jnp.int32, (group * tile, tile), 1)
    newer = column > row

    def contract(left, right, dims):
        return lax.dot_general(left, right, (dims, ((), ())), preferred_element_type=jnp.float32)

    def heads(ref, rows_here):
        return jnp.concatenate(
            [ref[rows_here, g * HEAD_WIDTH : (g + 1) * HEAD_WIDTH] for g in range(group)], axis=0
        )

    for start in range(0, rows, tile):
        here = slice(start, start + tile)
        band = slice(start, start + span)
        cosine = jnp.concatenate([cos_ref[here, :]] * group, axis=0)
        sine = jnp.concatenate([sin_ref[here, :]] * group, axis=0)
        raw = heads(raw_ref, here)
        shrink = lax.rsqrt(jnp.mean(raw * raw, axis=-1, keepdims=True) + norm_eps)
        normed = raw * shrink * gain
        query = (normed * cosine + pltpu.roll(normed, HEAD_WIDTH // 2, 1) * sine).astype(
            jnp.bfloat16
        )
        keys = key_ref[band, :]
        values = value_ref[band, :]
        given = heads(out_ref, here)
        bias = jnp.where(place + (start - WINDOW_LENGTH) + first_row >= 0, 0.0, -1e30)
        terms = jnp.exp2(contract(query, keys, ((1,), (1,))) * (scale * log2_e) + bias)
        terms = jnp.concatenate(
            [
                jnp.where(newer, terms[:, :tile], 0.0),
                terms[:, tile : span - tile],
                jnp.where(newer, 0.0, terms[:, span - tile :]),
            ],
            axis=1,
        )
        probs = terms * (1.0 / jnp.sum(terms, axis=-1, keepdims=True))
        weights = probs.astype(jnp.bfloat16)
        attended = contract(weights, values, ((1,), (0,))).astype(jnp.bfloat16)
        delta = jnp.sum(
            given.astype(jnp.float32) * attended.astype(jnp.float32), axis=-1, keepdims=True
        )
        prob_grads = contract(given, values, ((1,), (1,)))
        score_grads = (probs * (prob_grads - delta)).astype(jnp.bfloat16)
        grads = contract(score_grads, keys, ((1,), (0,))) * scale
        key_grad_ref[band, :] += contract(score_grads, query, ((0,), (0,))) * scale
        value_grad_ref[band, :] += contract(weights, given, ((0,), (0,)))
        unturned = grads * cosine + pltpu.roll(grads * sine, HEAD_WIDTH // 2, 1)
        scaled = unturned * gain
        back = shrink * (
            scaled
            - raw * (shrink * shrink) * jnp.mean(raw * scaled, axis=-1, keepdims=True)
        )
        for g in range(group):
            lanes = slice(g * HEAD_WIDTH, (g + 1) * HEAD_WIDTH)
            those = slice(g * tile, (g + 1) * tile)
            attended_ref[here, lanes] = attended[those]
            back_ref[here, lanes] = back[those].astype(jnp.bfloat16)
    for index, tile_ref in enumerate(tiles):
        for which, ref in enumerate((key_grad_ref, value_grad_ref)):
            tile_ref[which] = ref[index * rows : (index + 1) * rows, :].astype(tile_ref.dtype)


def band_attention(query_raw, bands, output_rows, cosine, sine, gain, heads_key):
    rows, width = query_raw.shape
    reach_back = len(bands) - 1
    span = rows * len(bands)
    wide = width // heads_key
    queries = pl.BlockSpec((rows, wide), lambda g: (0, g))
    pairs = pl.BlockSpec((2, rows, HEAD_WIDTH), lambda g: (0, 0, g))
    table = pl.BlockSpec((rows, HEAD_WIDTH), lambda g: (0, 0))
    kinds = [jnp.bfloat16] + [jnp.float32] * reach_back
    return pl.pallas_call(
        functools.partial(attention_kernel, reach_back),
        grid=(heads_key,),
        out_shape=[jax.ShapeDtypeStruct((rows, width), jnp.bfloat16)] * 2
        + [jax.ShapeDtypeStruct(bands[0].shape, kind) for kind in kinds],
        in_specs=[
            queries, queries, table, table, pl.BlockSpec((1, HEAD_WIDTH), lambda g: (0, 0)),
        ]
        + [pairs] * len(bands),
        out_specs=[queries, queries] + [pairs] * len(bands),
        scratch_shapes=[pltpu.VMEM((span, HEAD_WIDTH), jnp.bfloat16)] * 2
        + [pltpu.VMEM((span, HEAD_WIDTH), jnp.float32)] * 2,
        compiler_params=pltpu.CompilerParams(vmem_limit_bytes=56 * 2**20),
        cost_estimate=pl.CostEstimate(
            flops=10 * rows * span * width, bytes_accessed=16 * rows * width,
            transcendentals=rows * span * (width // HEAD_WIDTH),
        ),
    )(query_raw, output_rows, cosine, sine, gain, *bands)


def transposed(left_rows, right_rows):
    return lax.dot_general(
        left_rows, right_rows, (((1,), (1,)), ((), ())), preferred_element_type=jnp.float32
    )


def shards(tokens, query_weight, key_matrix, value_matrix, query_gain, key_norm_gain, cotangent):
    row_count = tokens.shape[0]
    heads_key = key_matrix.shape[1] // HEAD_WIDTH
    reach_back = WINDOW_LENGTH // row_count
    first_row = lax.axis_index("ctx") * row_count
    token_positions = (first_row + jnp.arange(row_count, dtype=jnp.int32)).astype(jnp.float32)
    query_columns, key_columns = query_weight.shape[1], key_matrix.shape[1]
    width = tokens.shape[1]
    size = lax.axis_size("ctx")
    shard = jnp.concatenate([query_weight, key_matrix, value_matrix], axis=1)
    inverse = jnp.power(
        jnp.float32(rope_base),
        -jnp.arange(0, HEAD_WIDTH, 2).astype(jnp.float32) / HEAD_WIDTH,
    )
    angles = token_positions[:, None] * inverse[None, :]
    cosine, sine = jnp.cos(angles), jnp.sin(angles)
    cosine = jnp.concatenate([cosine, cosine], axis=1)
    sine = jnp.concatenate([-sine, sine], axis=1)

    full_weight, turned_tokens, query_raw, key_raw, _, stacked = gather_and_project(
        shard, tokens, cosine, sine, key_norm_gain[None, :], 1
    )
    flat_weight = full_weight.reshape(width, shard.shape[1])

    def rotate_keys(unnormed_rows):
        return normalize_and_rotate(
            unnormed_rows, key_norm_gain, token_positions, heads_key, HEAD_WIDTH
        )

    _, key_pullback = jax.vjp(rotate_keys, key_raw)
    arrivals = []
    carried = stacked
    for hop_count in range(reach_back):
        carried = passed_along(carried, "ctx", 1)
        arrivals.append(carried)
    attended, query_back, *tiles = band_attention(
        query_raw, arrivals[::-1] + [stacked], cotangent, cosine, sine,
        query_gain[None, :], heads_key,
    )
    paired = lax.axis_size("tp") == 2
    weight_parts = [flat_weight]
    if paired:
        weight_parts = [flat_weight[: width // 2], flat_weight[width // 2 :]]
    query_terms = [transposed(query_back, part[:, :query_columns]) for part in weight_parts]
    returned = tiles[0]
    for hop_count in range(1, reach_back + 1):
        arrived = passed_along(returned.astype(jnp.bfloat16), "ctx", -1)
        if hop_count <= len(query_terms):
            arrived, query_terms[hop_count - 1] = lax.optimization_barrier(
                (arrived, query_terms[hop_count - 1])
            )
        returned = arrived.astype(jnp.float32) + tiles[hop_count]
    (key_backprop,) = key_pullback(returned[0])
    pair_back = jnp.concatenate([key_backprop, returned[1]], axis=1).astype(jnp.bfloat16)
    all_back = jnp.concatenate([query_back, pair_back], axis=1)
    token_terms = [
        (term + transposed(pair_back, part[:, query_columns:])).astype(jnp.bfloat16)
        for term, part in zip(query_terms, weight_parts)
    ]
    if paired:
        given = lax.ppermute(token_terms[0], "tp", [(0, 1), (1, 0)])
        gradient = weight_gradient(turned_tokens, all_back, 2)
        token_gradient = (
            token_terms[1].astype(jnp.float32) + given.astype(jnp.float32)
        ).astype(jnp.bfloat16)
    else:
        token_gradient = lax.psum_scatter(
            token_terms[0], "tp", scatter_dimension=1, tiled=True
        )
        gradient = weight_gradient(turned_tokens, all_back, 2)
    return (
        attended,
        token_gradient,
        gradient[:, :query_columns],
        gradient[:, query_columns : query_columns + key_columns],
        gradient[:, query_columns + key_columns :],
    )


def solution(mesh):
    in_specs = (
        P("ctx", None),
        P("ctx", "tp"),
        P("ctx", "tp"),
        P("ctx", "tp"),
        P(),
        P(),
        P("ctx", "tp"),
    )
    out_specs = (P("ctx", "tp"), P("ctx", "tp"), P("ctx", "tp"), P("ctx", "tp"), P("ctx", "tp"))
    return jax.shard_map(shards, mesh=mesh, in_specs=in_specs, out_specs=out_specs, check_vma=False)
```
